128 devices in a mesh: rep: 16 (over z_hi, y, core), tp: 8 (over x, z_lo).
Axes of the slice: x: 4, y: 4, z: 4 (z_hi: 2, z_lo: 2; z = z_hi * 2 + z_lo), core: 2. Of those that a mesh axis runs over, the one named last changes fastest.
Arguments:
- step_inputs: bfloat16 [2, 1024, 8192], P(None, 'rep', 'tp'), may hold values from -650 to 650
- norm_gain: bfloat16 [8192], replicated, may hold values from 0.25 to 1.75
- w_query: bfloat16 [8192, 4096], P(('rep', 'tp')), may hold values from -0.25 to 0.25
- w_key: bfloat16 [8192, 1024], P(('rep', 'tp')), may hold values from -0.0625 to 0.0625
- w_value: bfloat16 [8192, 1024], P(('rep', 'tp')), may hold values from -0.0625 to 0.0625
- w_out: bfloat16 [4096, 8192], P(('rep', 'tp')), may hold values from -0.375 to 0.375
- key_cache: bfloat16 [1024, 8, 512, 128], P('rep', 'tp'), may hold values from -420 to 420
- value_cache: bfloat16 [1024, 8, 512, 128], P('rep', 'tp'), may hold values from -6 to 6
- lengths: int32 [1024], P('rep'), may hold values from 128 to 512, as said below
Outputs:
- block_output: bfloat16 [2, 1024, 8192], P(None, 'rep', 'tp')
The draws below stay inside these ranges and needn't reach their ends.
Inputs may be any that keep to these rules, and one draw needn't show every extreme that they name: `lengths`: some row has exactly 512 cached positions.
All inputs are finite; a program needn't handle non-finite values.
Results may differ from the reference program's by a relative error of at most 0.012.
The reference program's roundings to bfloat16 on the way count: a program that leaves them out, or rounds other values in their place, can miss the bound.
Values may be sent and summed in bfloat16 or wider, within the bound.
No kernel may reach another device: no remote copies, remote signals or barrier semaphores. Data moves between devices by JAX's collectives and lax.ppermute only.
A program may use at most 192 MiB of HBM per device.

```python
import jax
import jax.numpy as jnp
from jax import lax

D = 8192
HQ = 32
KV = 8
HD = 128
L = 512
ROWS = 64
STEPS = 2
ROWS_ALL = 1024
N_REP = 16


def draw_step_inputs(key, part):
    key = jax.random.fold_in(key, 11)
    row_key, column_key, noise_key = jax.random.split(key, 3)
    row_scale = jnp.exp(jax.random.uniform(row_key, (STEPS, ROWS_ALL, 1), jnp.float32, 0.0, 2.4))
    column_scale = jnp.exp(jax.random.uniform(column_key, (1, 1, D), jnp.float32, 0.0, 2.4))
    noise = jnp.clip(jax.random.normal(noise_key, (STEPS, ROWS_ALL, D), jnp.float32), -5.0, 5.0)
    return (noise * row_scale * column_scale).astype(jnp.bfloat16)


def draw_key_cache(key, part):
    key = jax.random.fold_in(key, 23)
    noise_key = jax.random.fold_in(key, 0)
    noise = jnp.clip(jax.random.normal(noise_key, (ROWS_ALL, KV, L, HD), jnp.float32), -5.0, 5.0)
    return noise.astype(jnp.bfloat16)


def draw_lengths(key, part):
    key = jax.random.fold_in(key, 37)
    length_key, anchor_key = jax.random.split(key)
    lengths = jax.random.randint(length_key, (ROWS_ALL,), L // 4, L + 1)
    anchor = jax.random.randint(anchor_key, (), 0, ROWS_ALL)
    return lengths.at[anchor].set(L).astype(jnp.int32)


def with_spikes(drawn, own_key, source, target, shards_of, factor):
    owner, partner = [(jnp.arange(drawn.shape[axis_at]) // (drawn.shape[axis_at] // shards_of)).reshape([-1 if axis == axis_at else 1 for axis in range(drawn.ndim)]) for axis_at in (source, target)]
    chosen = jax.random.permutation(own_key, shards_of)[partner]
    strong = (owner == chosen) | (owner == (partner + shards_of // 2) % shards_of)
    return jnp.where(strong, factor * drawn, drawn)


def block_levels(key, extent, pieces, least, high):
    def one(axis_at, parts):
        heights = jax.random.uniform(jax.random.fold_in(jax.random.fold_in(key, 6), axis_at), (parts,), jnp.float32, least / len(pieces), high / len(pieces))
        return jnp.repeat(jnp.exp(heights), extent[axis_at] // parts).reshape((-1,) + (1,) * (len(extent) - axis_at - 1))

    gain = one(*pieces[0])
    for cut in pieces[1:]:
        gain = gain * one(*cut)
    return gain


def gaussian(rng, shape, spread, limit, shards=(), held_as=jnp.bfloat16):
    entries = jax.random.normal(rng, shape, jnp.float32) * spread
    if len(shards) > 0:
        entries = block_levels(rng, shape, shards, -0.22, 0.18) * entries
    return jnp.clip(entries, min=-limit, max=limit).astype(held_as)


def gaussian_with(key, shape, deviation, bound, cuts, heavy, held_as=jnp.bfloat16):
    entries = deviation * jax.random.normal(key, shape, jnp.float32)
    if cuts:
        entries = entries * block_levels(key, shape, cuts, -0.22, 0.18)
    return jnp.clip(with_spikes(entries, jax.random.fold_in(key, 3), *heavy), -bound, bound).astype(held_as)


def setup_inputs(seed: int = 0) -> dict:
    key_of = jax.random.split(jax.random.key(seed), 10)
    step_inputs = draw_step_inputs(jax.random.fold_in(key_of[9], 71), 0)
    norm_gain = jnp.clip(1.0 + 0.15 * jax.random.normal(key_of[1], (D,), jnp.float32), 0.25, 1.75).astype(jnp.bfloat16)
    w_query = gaussian_with(key_of[2], (D, HQ * HD), D ** -0.5, 0.25, ((0, 128),), (0, 1, 128, 5.5))
    w_key = gaussian(key_of[3], (D, KV * HD), D ** -0.5, 0.0625, ((0, 128),))
    w_value = gaussian(key_of[4], (D, KV * HD), D ** -0.5, 0.0625, ((0, 128),))
    w_out = gaussian_with(key_of[5], (HQ * HD, D), (HQ * HD) ** -0.5, 0.375, ((0, 128),), (0, 1, 128, 5.5))
    key_cache = draw_key_cache(jax.random.fold_in(key_of[9], 71), 0)
    value_cache = gaussian(key_of[7], (ROWS_ALL, KV, L, HD), 1.0, 6.0, ((0, 16), (1, 8)))
    lengths = draw_lengths(jax.random.fold_in(key_of[9], 71), 0)
    return dict(step_inputs=step_inputs, norm_gain=norm_gain, w_query=w_query, w_key=w_key, w_value=w_value, w_out=w_out, key_cache=key_cache, value_cache=value_cache, lengths=lengths)


norm_eps = 1e-05
rope_base = 500000.0

def rotate(vectors, positions):
    half_width = vectors.shape[-1] // 2
    ladder = jnp.arange(half_width).astype(jnp.float32)
    frequency = jnp.power(jnp.float32(rope_base), -2.0 * ladder / vectors.shape[-1])
    angles = positions.astype(jnp.float32)[:, None, None] * frequency[None, None, :]
    cosine_part = jnp.cos(angles)
    sine_part = jnp.sin(angles)
    leading = vectors[..., :half_width]
    trailing = vectors[..., half_width:]
    return jnp.concatenate([leading * cosine_part - trailing * sine_part, trailing * cosine_part + leading * sine_part], axis=-1)

def normalize(inputs, norm_gain):
    values = inputs.astype(jnp.float32)
    factor = lax.rsqrt(lax.optimization_barrier(jnp.mean(values * values, axis=-1, keepdims=True)) + norm_eps)
    return (values * factor * norm_gain.astype(jnp.float32)).astype(jnp.bfloat16)

def attend(queries, key_block, value_block, lengths_block, new_keys, new_values):
    row_count, head_count, head_width = queries.shape
    group_count = key_block.shape[1]
    score_scale = head_width ** (-0.5)
    grouped = queries.astype(jnp.float32).reshape(row_count, group_count, head_count // group_count, head_width)
    cache_scores = jnp.einsum('rkgd,rkld->rkgl', grouped, key_block.astype(jnp.float32)) * score_scale
    new_scores = jnp.einsum('rkgd,rksd->rkgs', grouped, new_keys.astype(jnp.float32)) * score_scale
    visible = jnp.arange(key_block.shape[2]).astype(jnp.int32)[None, :] < lengths_block[:, None]
    cache_scores = jnp.where(visible[:, None, None, :], cache_scores, -jnp.inf)
    highest = jnp.maximum(lax.optimization_barrier(jnp.max(cache_scores, axis=-1, keepdims=True)), lax.optimization_barrier(jnp.max(new_scores, axis=-1, keepdims=True)))
    cache_weights = jnp.exp(cache_scores - highest)
    new_weights = jnp.exp(new_scores - highest)
    denominator = lax.optimization_barrier(jnp.sum(cache_weights, axis=-1, keepdims=True)) + lax.optimization_barrier(jnp.sum(new_weights, axis=-1, keepdims=True))
    cache_probs = (cache_weights / denominator).astype(jnp.bfloat16)
    new_probs = (new_weights / denominator).astype(jnp.bfloat16)
    combined = jnp.einsum('rkgl,rkld->rkgd', cache_probs.astype(jnp.float32), value_block.astype(jnp.float32))
    combined = combined + jnp.einsum('rkgs,rksd->rkgd', new_probs.astype(jnp.float32), new_values.astype(jnp.float32))
    return combined.reshape(row_count, head_count * head_width).astype(jnp.bfloat16)

def reference(step_inputs, norm_gain, w_query, w_key, w_value, w_out, key_cache, value_cache, lengths):
    row_count = step_inputs.shape[1]
    kept_keys = []
    kept_values = []
    results = []
    for step_index in range(STEPS):
        normed = normalize(step_inputs[step_index], norm_gain)
        positions = lengths + step_index
        queries = jnp.dot(normed, w_query, preferred_element_type=jnp.float32).reshape(row_count, HQ, HD)
        queries = rotate(queries, positions).astype(jnp.bfloat16)
        fresh_key = jnp.dot(normed, w_key, preferred_element_type=jnp.float32).reshape(row_count, KV, HD)
        kept_keys.append(rotate(fresh_key, positions).astype(jnp.bfloat16))
        fresh_value = jnp.dot(normed, w_value, preferred_element_type=jnp.float32).astype(jnp.bfloat16)
        kept_values.append(fresh_value.reshape(row_count, KV, HD))
        new_keys = jnp.stack(kept_keys, axis=2)
        new_values = jnp.stack(kept_values, axis=2)
        blocks = (queries.reshape(N_REP, ROWS, HQ, HD), key_cache.reshape(N_REP, ROWS, KV, L, HD), value_cache.reshape(N_REP, ROWS, KV, L, HD), lengths.reshape(N_REP, ROWS), new_keys.reshape(N_REP, ROWS, KV, step_index + 1, HD), new_values.reshape(N_REP, ROWS, KV, step_index + 1, HD))
        attention = lax.map(lambda package: attend(*package), blocks).reshape(row_count, HQ * HD)
        results.append(jnp.dot(attention, w_out, preferred_element_type=jnp.float32).astype(jnp.bfloat16))
    return jnp.stack(results, axis=0)
```

```python
import functools

import jax
import jax.numpy as jnp
from jax import lax
from jax.experimental import pallas as pl
from jax.experimental.pallas import tpu as pltpu
from jax.sharding import Mesh, PartitionSpec as P

HD = 128
STEPS = 2
GROUP = 4

VMEM_BYTES = 60 * 1024 * 1024

norm_eps = 1e-05
rope_base = 500000.0

AXES = ("zh", "y1", "y0", "c", "x1", "x0", "zl")
REP = ("zh", "y1", "y0", "c")
TP = ("x1", "x0", "zl")
SPLIT = ("y1", "y0")
REST = "zh"


def pairs_of(change):
    pairs = []
    for device in range(128):
        bits = {axis: (device >> (6 - i)) & 1 for i, axis in enumerate(AXES)}
        moved = change(dict(bits))
        pairs.append((device, sum(moved[axis] << (6 - i) for i, axis in enumerate(AXES))))
    return pairs


def flipped(axis):
    def change(bits):
        bits[axis] ^= 1
        return bits

    return change


def permute(block, change):
    return lax.ppermute(block, AXES, pairs_of(change))


def shifted(high, low, by):
    def change(bits):
        place = (bits[high] * 2 + bits[low] + by) % 4
        bits[high], bits[low] = place >> 1, place & 1
        return bits

    return change


def ring_gather(block, pair, high, low):
    half = block.shape[0] // 2
    up, down = shifted(high, low, 1), shifted(high, low, -1)
    mate = permute(block, flipped(pair))
    own_side = [block, permute(block, up), permute(block, down)]
    mate_side = [mate, permute(mate, up), permute(mate, down)]
    for side in (own_side, mate_side):
        side.append(permute(side[1][:half], up))
        side.append(permute(side[2][half:], down))
    return own_side + mate_side


def ring_places(mine):
    return [mine, (mine + 3) % 4, (mine + 1) % 4, (mine + 2) % 4]


def turns(positions):
    half = HD // 2
    ladder = jnp.arange(half).astype(jnp.float32)
    frequency = jnp.power(jnp.float32(rope_base), -2.0 * ladder / HD)
    angles = positions.astype(jnp.float32)[:, None] * frequency[None, :]
    cosine, sine = jnp.cos(angles), jnp.sin(angles)
    return jnp.concatenate([cosine, cosine], axis=-1), jnp.concatenate([-sine, sine], axis=-1)


def settle(place, blocks, spots, sems):
    ring, pair = place[2], place[3]
    half = blocks[3].shape[0]
    copies = []
    for side in range(2):
        for k, spot in enumerate(ring_places(ring)):
            index = spot * 2 + (pair ^ side)
            first = side * 5 + k
            for low in range(1 if k < 3 else 2):
                rows = pl.ds(low * half, half if k == 3 else 2 * half)
                for source, target, sem in spots(blocks[first + low], index, rows, first + low):
                    copies.append(pltpu.make_async_copy(source, target, sems.at[sem]))
    for copy in copies:
        copy.start()
    return copies


def pack_kernel(query, key, value, out_weight, inputs, packed):
    rows = inputs.shape[0] // 8
    deep = out_weight.shape[0]
    wide, narrow = query.shape[1] // 8, key.shape[1] // 8
    width = inputs.shape[1]
    quarter = query.shape[0] // 4
    strip = width // 4
    for t in range(8):
        packed[t, :rows] = inputs[t * rows : (t + 1) * rows]
        packed[t, rows : rows + deep] = out_weight[:, t * width : (t + 1) * width]
        first = rows + deep
        for q in range(4):
            part = slice(q * quarter, (q + 1) * quarter)
            begin = q * strip
            for n in range(wide // strip):
                packed[t, first + n * quarter : first + (n + 1) * quarter, begin : begin + strip] = query[
                    part, t * wide + n * strip : t * wide + (n + 1) * strip
                ]
            last = slice(first + wide // strip * quarter, first + (wide // strip + 1) * quarter)
            packed[t, last, begin : begin + narrow] = key[part, t * narrow : (t + 1) * narrow]
            packed[t, last, begin + narrow : begin + strip] = value[part, t * narrow : (t + 1) * narrow]


def pack(query, key, value, out_weight, inputs):
    batch, width = inputs.shape
    depth = query.shape[0]
    rows = batch // 8 + out_weight.shape[0] + depth * 3 // 4
    vmem = pl.BlockSpec(memory_space=pltpu.VMEM)
    return pl.pallas_call(
        pack_kernel,
        out_shape=jax.ShapeDtypeStruct((8, rows, width), jnp.bfloat16),
        in_specs=[vmem] * 5,
        out_specs=vmem,
        compiler_params=pltpu.CompilerParams(vmem_limit_bytes=VMEM_BYTES),
    )(query, key, value, out_weight, inputs)


def unpack_kernel(packed, gain, normed, weight, out_weight):
    rows, width = normed.shape[2:]
    deep = out_weight.shape[0] // 8
    depth = weight.shape[0] // 8
    quarter, strip = depth // 4, width // 4
    total = None
    for t in range(8):
        values = packed[t, :rows].astype(jnp.float32)
        squares = jnp.sum(values * values, axis=-1, keepdims=True)
        total = squares if total is None else total + squares
    factor = lax.rsqrt(total / (8 * width) + norm_eps)
    for t in range(8):
        values = packed[t, :rows].astype(jnp.float32) * factor
        values = values * gain[t : t + 1, :].astype(jnp.float32)
        normed[t & 3, t >> 2] = values.astype(jnp.bfloat16)
        out_weight[t * deep : (t + 1) * deep] = packed[t, rows : rows + deep]
        first = rows + deep
        for n in range(3):
            for q in range(4):
                begin = t * depth + q * quarter
                weight[begin : begin + quarter, n * strip : (n + 1) * strip] = packed[
                    t, first + n * quarter : first + (n + 1) * quarter, q * strip : (q + 1) * strip
                ]


def unpack(packed, gain, rows, deep, depth):
    width = packed.shape[2]
    vmem = pl.BlockSpec(memory_space=pltpu.VMEM)
    return pl.pallas_call(
        unpack_kernel,
        out_shape=[
            jax.ShapeDtypeStruct((4, 2, rows, width), jnp.bfloat16),
            jax.ShapeDtypeStruct((8 * depth, width * 3 // 4), jnp.bfloat16),
            jax.ShapeDtypeStruct((8 * deep, width), jnp.bfloat16),
        ],
        in_specs=[vmem] * 2,
        out_specs=[vmem] * 3,
        compiler_params=pltpu.CompilerParams(vmem_limit_bytes=VMEM_BYTES),
    )(packed, gain)


def partial_kernel(place, *refs):
    blocks, weights, outs, acts, held, sums, sems, more = refs[:10], refs[10:14], refs[14:18], *refs[18:]

    width = blocks[0].shape[3]
    half = weights[0].shape[0]

    def spots(block, index, part, sem):
        return [
            (block.at[:, k], acts.at[part, index, :, pl.ds(k * width, width)], (sem, k)) for k in range(2)
        ]

    copies = settle(place, blocks, spots, sems)
    ring, core, rest = place[0], place[1], place[4]
    for i in range(4):
        first = ((rest ^ (i >> 1)) * 2 + (core ^ (i & 1))) * half
        copies.append(
            pltpu.make_async_copy(weights[i], held.at[pl.ds(pl.multiple_of(first, half), half)], more.at[i])
        )
        copies[-1].start()
    for copy in copies:
        copy.wait()
    batch = outs[0].shape[0]
    product = jnp.dot(acts[...].reshape(4 * batch, 2 * width), held[...], preferred_element_type=jnp.float32)
    sums[...] = product.astype(sums.dtype).reshape(sums.shape)
    for k in range(4):
        outs[k][...] = sums[ring ^ k]


def partial_products(place, blocks, weights):
    _, _, rows, width = blocks[0].shape
    depth, columns = weights[0].shape
    vmem = pl.BlockSpec(memory_space=pltpu.VMEM)
    return pl.pallas_call(
        partial_kernel,
        out_shape=[jax.ShapeDtypeStruct((8 * rows, columns), jnp.bfloat16)] * 4,
        in_specs=[pl.BlockSpec(memory_space=pltpu.SMEM)] + [pl.BlockSpec(memory_space=pl.ANY)] * 14,
        out_specs=[vmem] * 4,
        scratch_shapes=[
            pltpu.VMEM((4, 8, rows, 2 * width), jnp.bfloat16),
            pltpu.VMEM((4 * depth, columns), jnp.bfloat16),
            pltpu.VMEM((4, 8 * rows, columns), jnp.bfloat16),
            pltpu.SemaphoreType.DMA((10, 2)),
            pltpu.SemaphoreType.DMA((4,)),
        ],
        compiler_params=pltpu.CompilerParams(vmem_limit_bytes=VMEM_BYTES),
        cost_estimate=pl.CostEstimate(
            flops=2 * 32 * rows * 2 * width * columns, bytes_accessed=8 * 1024 * 1024, transcendentals=0
        ),
    )(place, *blocks, *weights)


def output_kernel(place, *refs):
    blocks, weight, out, acts, held, sems, more = refs[:10], *refs[10:]
    width = blocks[0].shape[1]

    def spots(block, index, part, sem):
        columns = pl.ds(pl.multiple_of(index * width, width), width)
        return [(block, acts.at[part, columns], (sem,))]

    copies = settle(place, blocks, spots, more)
    for group in range(8):
        rows = pl.ds(group * width, width)
        copies.append(pltpu.make_async_copy(weight.at[rows], held.at[rows], sems.at[group]))
        copies[-1].start()
    for copy in copies:
        copy.wait()
    out[...] = jnp.dot(acts[...], held[...], preferred_element_type=jnp.float32).astype(out.dtype)


def output_product(place, blocks, weight):
    batch, width = blocks[0].shape
    columns = weight.shape[1]
    return pl.pallas_call(
        output_kernel,
        out_shape=jax.ShapeDtypeStruct((batch, columns), jnp.bfloat16),
        in_specs=[pl.BlockSpec(memory_space=pltpu.SMEM)] + [pl.BlockSpec(memory_space=pl.ANY)] * 11,
        out_specs=pl.BlockSpec(memory_space=pltpu.VMEM),
        scratch_shapes=[
            pltpu.VMEM((batch, 8 * width), jnp.bfloat16),
            pltpu.VMEM((8 * width, columns), jnp.bfloat16),
            pltpu.SemaphoreType.DMA((8,)),
            pltpu.SemaphoreType.DMA((10,)),
        ],
        compiler_params=pltpu.CompilerParams(vmem_limit_bytes=VMEM_BYTES),
        cost_estimate=pl.CostEstimate(
            flops=2 * batch * 8 * width * columns, bytes_accessed=10 * 1024 * 1024, transcendentals=0
        ),
    )(place, *blocks, weight)


def tie(block, *others):
    anywhere = pl.BlockSpec(memory_space=pl.ANY)

    def kernel(*refs):
        pass

    return pl.pallas_call(
        kernel,
        out_shape=jax.ShapeDtypeStruct(block.shape, block.dtype),
        in_specs=[anywhere] * (1 + len(others)),
        out_specs=anywhere,
        input_output_aliases={0: 0},
    )(block, *others)


def attention_kernel(lengths, *refs):
    parts, (cosine, sine, key, value, out), scratch = refs[:4], refs[4:9], refs[9:]
    queries, fresh_keys, fresh_values, scores, sums = scratch
    rows, heads, _ = queries.shape
    chunk = key.shape[0]
    step = pl.program_id(0)

    @pl.when(step == 0)
    def _():
        projected = parts[0][...].astype(jnp.float32)
        for part in parts[1:]:
            projected = projected + part[...].astype(jnp.float32)

        def head(k):
            return projected[:, k * HD : (k + 1) * HD]

        def turned(vectors):
            moved = vectors * cosine[...] + pltpu.roll(vectors, HD // 2, 1) * sine[...]
            return moved.astype(jnp.bfloat16).astype(jnp.float32)

        for k in range(GROUP):
            query = turned(head(k))
            for s in range(STEPS):
                queries[:, s * GROUP + k, :] = query[s * rows : (s + 1) * rows]
        fresh_key = turned(head(GROUP))
        fresh_value = head(GROUP + 1).astype(jnp.bfloat16).astype(jnp.float32)
        for s in range(STEPS):
            fresh_keys[s] = fresh_key[s * rows : (s + 1) * rows]
            fresh_values[s] = fresh_value[s * rows : (s + 1) * rows]

    scale = HD ** (-0.5)
    here = pl.ds(pl.multiple_of(step * chunk, chunk), chunk)
    query = queries[here].reshape(chunk * heads, HD)
    for r in range(chunk):
        scores[r * heads : (r + 1) * heads] = lax.dot_general(
            query[r * heads : (r + 1) * heads].astype(jnp.bfloat16),
            key[r],
            (((1,), (1,)), ((), ())),
            preferred_element_type=jnp.float32,
        )
    cached = scores[...] * scale
    spot = lax.broadcasted_iota(jnp.int32, cached.shape, 1)
    cached = jnp.where(spot < lengths[...], cached, -jnp.inf)
    at_step = lax.broadcasted_iota(jnp.int32, (chunk * heads, 1), 0) % heads // GROUP

    def repeated(vectors):
        return jnp.broadcast_to(vectors[:, None, :], (chunk, heads, HD)).reshape(chunk * heads, HD)

    new = []
    highest = jnp.max(cached, axis=-1, keepdims=True)
    for s in range(STEPS):
        score = jnp.sum(query * repeated(fresh_keys[s, here]), axis=-1, keepdims=True) * scale
        new.append(jnp.where(at_step >= s, score, -jnp.inf))
        highest = jnp.maximum(highest, new[s])
    cached = jnp.exp(cached - highest)
    new = [jnp.exp(score - highest) for score in new]
    total = jnp.sum(cached, axis=-1, keepdims=True) + new[0] + new[1]
    share = 1.0 / total
    scores[...] = cached * share
    result = None
    for s in range(STEPS):
        prob = (new[s] * share).astype(jnp.bfloat16).astype(jnp.float32)
        term = prob * repeated(fresh_values[s, here])
        result = term if result is None else result + term
    result = result.reshape(chunk, heads, HD)
    for r in range(chunk):
        prob = scores[r * heads : (r + 1) * heads].astype(jnp.bfloat16)
        sums[step * chunk + r] = result[r] + jnp.dot(prob, value[r], preferred_element_type=jnp.float32)

    @pl.when(step == pl.num_programs(0) - 1)
    def _():
        for s in range(STEPS):
            for k in range(GROUP):
                out[s * rows : (s + 1) * rows, k * HD : (k + 1) * HD] = sums[:, s * GROUP + k, :].astype(out.dtype)


def attention_of(parts, cosine, sine, key_cache, value_cache, lengths, chunk=8):
    batch, columns = parts[0].shape
    rows, spots, _ = key_cache.shape
    heads = STEPS * GROUP
    whole = lambda *shape: pl.BlockSpec(shape, lambda i: (0,) * len(shape))
    cache = pl.BlockSpec((chunk, spots, HD), lambda i: (i, 0, 0))
    return pl.pallas_call(
        attention_kernel,
        grid=(rows // chunk,),
        out_shape=jax.ShapeDtypeStruct((batch, GROUP * HD), jnp.bfloat16),
        in_specs=[pl.BlockSpec((chunk * heads, 1), lambda i: (i, 0))]
        + [whole(batch, columns)] * 4
        + [whole(batch, HD), whole(batch, HD), cache, cache],
        out_specs=whole(batch, GROUP * HD),
        scratch_shapes=[
            pltpu.VMEM((rows, heads, HD), jnp.float32),
            pltpu.VMEM((STEPS, rows, HD), jnp.float32),
            pltpu.VMEM((STEPS, rows, HD), jnp.float32),
            pltpu.VMEM((chunk * heads, spots), jnp.float32),
            pltpu.VMEM((rows, heads, HD), jnp.float32),
        ],
        compiler_params=pltpu.CompilerParams(
            vmem_limit_bytes=VMEM_BYTES, dimension_semantics=("arbitrary",)
        ),
        cost_estimate=pl.CostEstimate(
            flops=4 * rows * heads * spots * HD,
            bytes_accessed=4 * rows * spots * HD,
            transcendentals=rows * heads * spots,
        ),
    )(jnp.repeat(lengths, heads)[:, None], *parts, cosine, sine, key_cache, value_cache)


def shards(step_inputs, norm_gain, w_query, w_key, w_value, w_out, key_cache, value_cache, lengths):
    steps, rows, width = step_inputs.shape
    batch = steps * rows
    place = jnp.stack(
        [
            lax.axis_index(("y1", "y0")),
            lax.axis_index("c"),
            lax.axis_index(("x1", "x0")),
            lax.axis_index("zl"),
            lax.axis_index("zh"),
        ]
    ).astype(jnp.int32)

    packed = pack(w_query, w_key, w_value, w_out, step_inputs.reshape(batch, width))
    packed = lax.all_to_all(packed, TP, 0, 0, tiled=True)
    normed, mine, out_mine = unpack(
        packed, norm_gain.reshape(8, width), batch // 8, w_out.shape[0], w_query.shape[0]
    )
    far = permute(mine, flipped(REST))
    weights = (mine, permute(mine, flipped("c")), far, permute(far, flipped("c")))
    out_weight = lax.all_gather(out_mine, REP, axis=0, tiled=True)

    moved = lax.all_to_all(normed, SPLIT, 0, 0, tiled=True)
    gathered = ring_gather(moved, "zl", "x1", "x0")
    partial = partial_products(place, gathered, weights)
    changes = [flipped(SPLIT[0]), flipped(SPLIT[1])]
    parts = [
        partial[0],
        permute(partial[3], lambda bits: changes[0](changes[1](bits))),
        permute(partial[2], changes[0]),
        permute(partial[1], changes[1]),
    ]
    positions = (lengths[None, :] + jnp.arange(steps)[:, None]).reshape(batch)
    cosine, sine = turns(positions)
    attention = attention_of(
        parts, cosine, sine, key_cache[:, 0], value_cache[:, 0], lengths
    )
    joined = ring_gather(attention, "zl", "x1", "x0")
    result = output_product(place, joined, out_weight)
    return result.reshape(steps, rows, width)


def solution(mesh):
    fine = Mesh(mesh.devices.reshape((2,) * 7), AXES)
    in_specs = (
        P(None, REP, TP),
        P(),
        P(AXES, None),
        P(AXES, None),
        P(AXES, None),
        P(AXES, None),
        P(REP, TP, None, None),
        P(REP, TP, None, None),
        P(REP),
    )
    out_specs = P(None, REP, TP)
    return jax.shard_map(shards, mesh=fine, in_specs=in_specs, out_specs=out_specs, check_vma=False)
```

```python
import functools

import jax
import jax.numpy as jnp
from jax import lax
from jax.experimental import pallas as pl
from jax.experimental.pallas import tpu as pltpu
from jax.sharding import Mesh, PartitionSpec as P

HD = 128
STEPS = 2
GROUP = 4

VMEM_BYTES = 60 * 1024 * 1024

norm_eps = 1e-05
rope_base = 500000.0

AXES = ("zh", "y1", "y0", "c", "x1", "x0", "zl")
REP = ("zh", "y1", "y0", "c")
TP = ("x1", "x0", "zl")
SPLIT = ("zh", "y0")
REST = "y1"


def pairs_of(change):
    pairs = []
    for device in range(128):
        bits = {axis: (device >> (6 - i)) & 1 for i, axis in enumerate(AXES)}
        moved = change(dict(bits))
        pairs.append((device, sum(moved[axis] << (6 - i) for i, axis in enumerate(AXES))))
    return pairs


def flipped(axis):
    def change(bits):
        bits[axis] ^= 1
        return bits

    return change


def permute(block, change):
    return lax.ppermute(block, AXES, pairs_of(change))


def shifted(high, low, by):
    def change(bits):
        place = (bits[high] * 2 + bits[low] + by) % 4
        bits[high], bits[low] = place >> 1, place & 1
        return bits

    return change


def ring_gather(block, pair, high, low):
    half = block.shape[0] // 2
    up, down = shifted(high, low, 1), shifted(high, low, -1)
    mate = permute(block, flipped(pair))
    own_side = [block, permute(block, up), permute(block, down)]
    mate_side = [mate, permute(mate, up), permute(mate, down)]
    for side in (own_side, mate_side):
        side.append(permute(side[1][:half], up))
        side.append(permute(side[2][half:], down))
    return own_side + mate_side


def ring_places(mine):
    return [mine, (mine + 3) % 4, (mine + 1) % 4, (mine + 2) % 4]


def turns(positions):
    half = HD // 2
    ladder = jnp.arange(half).astype(jnp.float32)
    frequency = jnp.power(jnp.float32(rope_base), -2.0 * ladder / HD)
    angles = positions.astype(jnp.float32)[:, None] * frequency[None, :]
    cosine, sine = jnp.cos(angles), jnp.sin(angles)
    return jnp.concatenate([cosine, cosine], axis=-1), jnp.concatenate([-sine, sine], axis=-1)


def settle(place, blocks, spots, sems):
    ring, pair = place[2], place[3]
    half = blocks[3].shape[0]
    copies = []
    for side in range(2):
        for k, spot in enumerate(ring_places(ring)):
            index = spot * 2 + (pair ^ side)
            first = side * 5 + k
            for low in range(1 if k < 3 else 2):
                rows = pl.ds(low * half, half if k == 3 else 2 * half)
                for source, target, sem in spots(blocks[first + low], index, rows, first + low):
                    copies.append(pltpu.make_async_copy(source, target, sems.at[sem]))
    for copy in copies:
        copy.start()
    return copies


def pack_kernel(query, key, value, out_weight, inputs, packed):
    rows = inputs.shape[0] // 8
    deep = out_weight.shape[0]
    wide, narrow = query.shape[1] // 8, key.shape[1] // 8
    width = inputs.shape[1]
    quarter = query.shape[0] // 4
    strip = width // 4
    for t in range(8):
        packed[t, :rows] = inputs[t * rows : (t + 1) * rows]
        packed[t, rows : rows + deep] = out_weight[:, t * width : (t + 1) * width]
        first = rows + deep
        for q in range(4):
            part = slice(q * quarter, (q + 1) * quarter)
            begin = q * strip
            for n in range(wide // strip):
                packed[t, first + n * quarter : first + (n + 1) * quarter, begin : begin + strip] = query[
                    part, t * wide + n * strip : t * wide + (n + 1) * strip
                ]
            last = slice(first + wide // strip * quarter, first + (wide // strip + 1) * quarter)
            packed[t, last, begin : begin + narrow] = key[part, t * narrow : (t + 1) * narrow]
            packed[t, last, begin + narrow : begin + strip] = value[part, t * narrow : (t + 1) * narrow]


def pack(query, key, value, out_weight, inputs):
    batch, width = inputs.shape
    depth = query.shape[0]
    rows = batch // 8 + out_weight.shape[0] + depth * 3 // 4
    vmem = pl.BlockSpec(memory_space=pltpu.VMEM)
    return pl.pallas_call(
        pack_kernel,
        out_shape=jax.ShapeDtypeStruct((8, rows, width), jnp.bfloat16),
        in_specs=[vmem] * 5,
        out_specs=vmem,
        compiler_params=pltpu.CompilerParams(vmem_limit_bytes=VMEM_BYTES),
    )(query, key, value, out_weight, inputs)


def unpack_kernel(packed, gain, normed, weight, out_weight):
    rows, width = normed.shape[2:]
    deep = out_weight.shape[0] // 8
    depth = weight.shape[0] // 8
    quarter, strip = depth // 4, width // 4
    total = None
    for t in range(8):
        values = packed[t, :rows].astype(jnp.float32)
        squares = jnp.sum(values * values, axis=-1, keepdims=True)
        total = squares if total is None else total + squares
    factor = lax.rsqrt(total / (8 * width) + norm_eps)
    for t in range(8):
        values = packed[t, :rows].astype(jnp.float32) * factor
        values = values * gain[t : t + 1, :].astype(jnp.float32)
        normed[(t >> 2) * 2 + (t & 1), (t >> 1) & 1] = values.astype(jnp.bfloat16)
        out_weight[t * deep : (t + 1) * deep] = packed[t, rows : rows + deep]
        first = rows + deep
        for n in range(3):
            for q in range(4):
                begin = t * depth + q * quarter
                weight[begin : begin + quarter, n * strip : (n + 1) * strip] = packed[
                    t, first + n * quarter : first + (n + 1) * quarter, q * strip : (q + 1) * strip
                ]


def unpack(packed, gain, rows, deep, depth):
    width = packed.shape[2]
    vmem = pl.BlockSpec(memory_space=pltpu.VMEM)
    return pl.pallas_call(
        unpack_kernel,
        out_shape=[
            jax.ShapeDtypeStruct((4, 2, rows, width), jnp.bfloat16),
            jax.ShapeDtypeStruct((8 * depth, width * 3 // 4), jnp.bfloat16),
            jax.ShapeDtypeStruct((8 * deep, width), jnp.bfloat16),
        ],
        in_specs=[vmem] * 2,
        out_specs=[vmem] * 3,
        compiler_params=pltpu.CompilerParams(vmem_limit_bytes=VMEM_BYTES),
    )(packed, gain)


def partial_kernel(place, *refs):
    blocks, weights, outs, acts, held, sums, sems, more = refs[:10], refs[10:14], refs[14:18], *refs[18:]

    width = blocks[0].shape[3]
    half = weights[0].shape[0]

    def spots(block, index, part, sem):
        return [
            (block.at[:, k], acts.at[part, index, :, pl.ds(k * width, width)], (sem, k)) for k in range(2)
        ]

    copies = settle(place, blocks, spots, sems)
    here, core, rest = place[4] * 2 + place[0] % 2, place[1], place[0] // 2
    for i in range(4):
        first = ((rest ^ (i >> 1)) * 2 + (core ^ (i & 1))) * half
        copies.append(
            pltpu.make_async_copy(weights[i], held.at[pl.ds(pl.multiple_of(first, half), half)], more.at[i])
        )
        copies[-1].start()
    for copy in copies:
        copy.wait()
    batch = outs[0].shape[0]
    product = jnp.dot(acts[...].reshape(4 * batch, 2 * width), held[...], preferred_element_type=jnp.float32)
    sums[...] = product.astype(sums.dtype).reshape(sums.shape)
    for k in range(4):
        outs[k][...] = sums[here ^ k]


def partial_products(place, blocks, weights):
    _, _, rows, width = blocks[0].shape
    depth, columns = weights[0].shape
    vmem = pl.BlockSpec(memory_space=pltpu.VMEM)
    return pl.pallas_call(
        partial_kernel,
        out_shape=[jax.ShapeDtypeStruct((8 * rows, columns), jnp.bfloat16)] * 4,
        in_specs=[pl.BlockSpec(memory_space=pltpu.SMEM)] + [pl.BlockSpec(memory_space=pl.ANY)] * 14,
        out_specs=[vmem] * 4,
        scratch_shapes=[
            pltpu.VMEM((4, 8, rows, 2 * width), jnp.bfloat16),
            pltpu.VMEM((4 * depth, columns), jnp.bfloat16),
            pltpu.VMEM((4, 8 * rows, columns), jnp.bfloat16),
            pltpu.SemaphoreType.DMA((10, 2)),
            pltpu.SemaphoreType.DMA((4,)),
        ],
        compiler_params=pltpu.CompilerParams(vmem_limit_bytes=VMEM_BYTES),
        cost_estimate=pl.CostEstimate(
            flops=2 * 32 * rows * 2 * width * columns, bytes_accessed=8 * 1024 * 1024, transcendentals=0
        ),
    )(place, *blocks, *weights)


def output_kernel(place, *refs):
    blocks, weight, out, acts, sems = refs[:10], *refs[10:]
    width = blocks[0].shape[1]

    def spots(block, index, part, sem):
        columns = pl.ds(pl.multiple_of(index * width, width), width)
        return [(block, acts.at[part, columns], (sem,))]

    for copy in settle(place, blocks, spots, sems):
        copy.wait()
    out[...] = jnp.dot(acts[...], weight[...], preferred_element_type=jnp.float32).astype(out.dtype)


def output_product(place, blocks, weight):
    batch, width = blocks[0].shape
    columns = weight.shape[1]
    return pl.pallas_call(
        output_kernel,
        out_shape=jax.ShapeDtypeStruct((batch, columns), jnp.bfloat16),
        in_specs=[pl.BlockSpec(memory_space=pltpu.SMEM)]
        + [pl.BlockSpec(memory_space=pl.ANY)] * 10
        + [pl.BlockSpec(memory_space=pltpu.VMEM)],
        out_specs=pl.BlockSpec(memory_space=pltpu.VMEM),
        scratch_shapes=[
            pltpu.VMEM((batch, 8 * width), jnp.bfloat16),
            pltpu.SemaphoreType.DMA((10,)),
        ],
        compiler_params=pltpu.CompilerParams(vmem_limit_bytes=32 * 1024 * 1024),
        cost_estimate=pl.CostEstimate(
            flops=2 * batch * 8 * width * columns, bytes_accessed=10 * 1024 * 1024, transcendentals=0
        ),
    )(place, *blocks, weight)


def tie(block, *others):
    anywhere = pl.BlockSpec(memory_space=pl.ANY)

    def kernel(*refs):
        pass

    return pl.pallas_call(
        kernel,
        out_shape=jax.ShapeDtypeStruct(block.shape, block.dtype),
        in_specs=[anywhere] * (1 + len(others)),
        out_specs=anywhere,
        input_output_aliases={0: 0},
    )(block, *others)


def stage_kernel(count, arrays, *refs):
    sources, targets, sems = refs[:arrays], refs[count:-1], refs[-1]
    copies = []
    for i in range(arrays):
        pieces = sems.shape[1]
        size = sources[i].shape[0] // pieces
        for k in range(pieces):
            part = pl.ds(k * size, size)
            copies.append(pltpu.make_async_copy(sources[i].at[part], targets[i].at[part], sems.at[i, k]))
    for copy in copies:
        copy.start()
    for copy in copies:
        copy.wait()


def stage(arrays, *others):
    anywhere = pl.BlockSpec(memory_space=pl.ANY)
    count = len(arrays) + len(others)
    size = sum(array.size * array.dtype.itemsize for array in arrays)
    return pl.pallas_call(
        functools.partial(stage_kernel, count, len(arrays)),
        out_shape=[jax.ShapeDtypeStruct(array.shape, array.dtype) for array in arrays],
        in_specs=[anywhere] * count,
        out_specs=[anywhere] * len(arrays),
        scratch_shapes=[pltpu.SemaphoreType.DMA((len(arrays), 8))],
        compiler_params=pltpu.CompilerParams(vmem_limit_bytes=1024 * 1024),
        cost_estimate=pl.CostEstimate(flops=0, bytes_accessed=2 * size, transcendentals=0),
    )(*arrays, *others)


def attention_kernel(lengths, *refs):
    parts, (cosine, sine, key, value, out), scratch = refs[:4], refs[4:9], refs[9:]
    queries, fresh_keys, fresh_values, scores, sums = scratch
    rows, heads, _ = queries.shape
    chunk = scores.shape[0] // heads

    if True:
        projected = parts[0][...].astype(jnp.float32)
        for part in parts[1:]:
            projected = projected + part[...].astype(jnp.float32)

        def head(k):
            return projected[:, k * HD : (k + 1) * HD]

        def turned(vectors):
            moved = vectors * cosine[...] + pltpu.roll(vectors, HD // 2, 1) * sine[...]
            return moved.astype(jnp.bfloat16).astype(jnp.float32)

        for k in range(GROUP):
            query = turned(head(k))
            for s in range(STEPS):
                queries[:, s * GROUP + k, :] = query[s * rows : (s + 1) * rows]
        fresh_key = turned(head(GROUP))
        fresh_value = head(GROUP + 1).astype(jnp.bfloat16).astype(jnp.float32)
        for s in range(STEPS):
            fresh_keys[s] = fresh_key[s * rows : (s + 1) * rows]
            fresh_values[s] = fresh_value[s * rows : (s + 1) * rows]

    scale = HD ** (-0.5)
    at_step = lax.broadcasted_iota(jnp.int32, (chunk * heads, 1), 0) % heads // GROUP

    def repeated(vectors):
        return jnp.broadcast_to(vectors[:, None, :], (chunk, heads, HD)).reshape(chunk * heads, HD)

    def some_rows(step, carry):
        begin = pl.multiple_of(step * chunk, chunk)
        here = pl.ds(begin, chunk)
        query = queries[here].reshape(chunk * heads, HD)
        for r in range(chunk):
            scores[r * heads : (r + 1) * heads] = lax.dot_general(
                query[r * heads : (r + 1) * heads].astype(jnp.bfloat16),
                key[begin + r],
                (((1,), (1,)), ((), ())),
                preferred_element_type=jnp.float32,
            )
        cached = scores[...] * scale
        spot = lax.broadcasted_iota(jnp.int32, cached.shape, 1)
        limit = lengths[pl.ds(pl.multiple_of(step * chunk * heads, chunk * heads), chunk * heads)]
        cached = jnp.where(spot < limit, cached, -jnp.inf)
        new = []
        highest = jnp.max(cached, axis=-1, keepdims=True)
        for s in range(STEPS):
            score = jnp.sum(query * repeated(fresh_keys[s, here]), axis=-1, keepdims=True) * scale
            new.append(jnp.where(at_step >= s, score, -jnp.inf))
            highest = jnp.maximum(highest, new[s])
        cached = jnp.exp(cached - highest)
        new = [jnp.exp(score - highest) for score in new]
        total = jnp.sum(cached, axis=-1, keepdims=True) + new[0] + new[1]
        share = 1.0 / total
        scores[...] = cached * share
        result = None
        for s in range(STEPS):
            prob = (new[s] * share).astype(jnp.bfloat16).astype(jnp.float32)
            term = prob * repeated(fresh_values[s, here])
            result = term if result is None else result + term
        result = result.reshape(chunk, heads, HD)
        for r in range(chunk):
            prob = scores[r * heads : (r + 1) * heads].astype(jnp.bfloat16)
            sums[begin + r] = result[r] + jnp.dot(prob, value[begin + r], preferred_element_type=jnp.float32)
        return carry

    lax.fori_loop(0, rows // chunk, some_rows, 0)
    for s in range(STEPS):
        for k in range(GROUP):
            out[s * rows : (s + 1) * rows, k * HD : (k + 1) * HD] = sums[:, s * GROUP + k, :].astype(out.dtype)


def attention_of(parts, cosine, sine, key_cache, value_cache, lengths, chunk=8):
    batch, columns = parts[0].shape
    rows, spots, _ = key_cache.shape
    heads = STEPS * GROUP
    vmem = pl.BlockSpec(memory_space=pltpu.VMEM)
    return pl.pallas_call(
        attention_kernel,
        out_shape=jax.ShapeDtypeStruct((batch, GROUP * HD), jnp.bfloat16),
        in_specs=[vmem] * 9,
        out_specs=vmem,
        scratch_shapes=[
            pltpu.VMEM((rows, heads, HD), jnp.float32),
            pltpu.VMEM((STEPS, rows, HD), jnp.float32),
            pltpu.VMEM((STEPS, rows, HD), jnp.float32),
            pltpu.VMEM((chunk * heads, spots), jnp.float32),
            pltpu.VMEM((rows, heads, HD), jnp.float32),
        ],
        compiler_params=pltpu.CompilerParams(vmem_limit_bytes=32 * 1024 * 1024),
        cost_estimate=pl.CostEstimate(
            flops=4 * rows * heads * spots * HD,
            bytes_accessed=4 * rows * spots * HD,
            transcendentals=rows * heads * spots,
        ),
    )(jnp.repeat(lengths, heads)[:, None], *parts, cosine, sine, key_cache, value_cache)


def shards(step_inputs, norm_gain, w_query, w_key, w_value, w_out, key_cache, value_cache, lengths):
    steps, rows, width = step_inputs.shape
    batch = steps * rows
    place = jnp.stack(
        [
            lax.axis_index(("y1", "y0")),
            lax.axis_index("c"),
            lax.axis_index(("x1", "x0")),
            lax.axis_index("zl"),
            lax.axis_index("zh"),
        ]
    ).astype(jnp.int32)

    packed = pack(w_query, w_key, w_value, w_out, step_inputs.reshape(batch, width))
    packed = lax.all_to_all(packed, TP, 0, 0, tiled=True)
    normed, mine, out_mine = unpack(
        packed, norm_gain.reshape(8, width), batch // 8, w_out.shape[0], w_query.shape[0]
    )
    out_weight = lax.all_gather(out_mine, REP, axis=0, tiled=True)

    moved = lax.all_to_all(normed, SPLIT, 0, 0, tiled=True)
    mine = tie(mine, moved)
    far = permute(mine, flipped(REST))
    gathered = ring_gather(moved, "zl", "x1", "x0")
    far = tie(far, gathered[3], gathered[4], gathered[6], gathered[7])
    weights = (mine, permute(mine, flipped("c")), far, permute(far, flipped("c")))
    partial = partial_products(place, gathered, weights)
    caches = stage((key_cache[:, 0], value_cache[:, 0]), partial[0])
    changes = [flipped(SPLIT[0]), flipped(SPLIT[1])]
    parts = [
        partial[0],
        permute(partial[3], lambda bits: changes[0](changes[1](bits))),
        permute(partial[2], changes[0]),
        permute(partial[1], changes[1]),
    ]
    positions = (lengths[None, :] + jnp.arange(steps)[:, None]).reshape(batch)
    cosine, sine = turns(positions)
    attention = attention_of(
        parts, cosine, sine, *caches, lengths
    )
    joined = ring_gather(attention, "zl", "x1", "x0")
    out_weight = stage((out_weight,), attention)[0]
    result = output_product(place, joined, out_weight)
    return result.reshape(steps, rows, width)


def solution(mesh):
    fine = Mesh(mesh.devices.reshape((2,) * 7), AXES)
    in_specs = (
        P(None, REP, TP),
        P(),
        P(AXES, None),
        P(AXES, None),
        P(AXES, None),
        P(AXES, None),
        P(REP, TP, None, None),
        P(REP, TP, None, None),
        P(REP),
    )
    out_specs = P(None, REP, TP)
    return jax.shard_map(shards, mesh=fine, in_specs=in_specs, out_specs=out_specs, check_vma=False)
```

```python
import functools

import jax
import jax.numpy as jnp
from jax import lax
from jax.experimental import pallas as pl
from jax.experimental.pallas import tpu as pltpu
from jax.sharding import Mesh, PartitionSpec as P

HD = 128
STEPS = 2
GROUP = 4

VMEM_BYTES = 60 * 1024 * 1024

norm_eps = 1e-05
rope_base = 500000.0

AXES = ("zh", "y1", "y0", "c", "x1", "x0", "zl")
REP = ("zh", "y1", "y0", "c")
TP = ("x1", "x0", "zl")
SPLIT = ("zh", "y0")
REST = "y1"


def pairs_of(change):
    pairs = []
    for device in range(128):
        bits = {axis: (device >> (6 - i)) & 1 for i, axis in enumerate(AXES)}
        moved = change(dict(bits))
        pairs.append((device, sum(moved[axis] << (6 - i) for i, axis in enumerate(AXES))))
    return pairs


def flipped(axis):
    def change(bits):
        bits[axis] ^= 1
        return bits

    return change


def permute(block, change):
    return lax.ppermute(block, AXES, pairs_of(change))


def shifted(high, low, by):
    def change(bits):
        place = (bits[high] * 2 + bits[low] + by) % 4
        bits[high], bits[low] = place >> 1, place & 1
        return bits

    return change


def ring_gather(block, pair, high, low):
    half = block.shape[0] // 2
    up, down = shifted(high, low, 1), shifted(high, low, -1)
    mate = permute(block, flipped(pair))
    own_side = [block, permute(block, up), permute(block, down)]
    mate_side = [mate, permute(mate, up), permute(mate, down)]
    for side in (own_side, mate_side):
        side.append(permute(side[1][:half], up))
        side.append(permute(side[2][half:], down))
    return own_side + mate_side


def ring_places(mine):
    return [mine, (mine + 3) % 4, (mine + 1) % 4, (mine + 2) % 4]


def turns(positions):
    half = HD // 2
    ladder = jnp.arange(half).astype(jnp.float32)
    frequency = jnp.power(jnp.float32(rope_base), -2.0 * ladder / HD)
    angles = positions.astype(jnp.float32)[:, None] * frequency[None, :]
    cosine, sine = jnp.cos(angles), jnp.sin(angles)
    return jnp.concatenate([cosine, cosine], axis=-1), jnp.concatenate([-sine, sine], axis=-1)


def settle(place, blocks, spots, sems):
    ring, pair = place[2], place[3]
    half = blocks[3].shape[0]
    copies = []
    for side in range(2):
        for k, spot in enumerate(ring_places(ring)):
            index = spot * 2 + (pair ^ side)
            first = side * 5 + k
            for low in range(1 if k < 3 else 2):
                rows = pl.ds(low * half, half if k == 3 else 2 * half)
                for source, target, sem in spots(blocks[first + low], index, rows, first + low):
                    copies.append(pltpu.make_async_copy(source, target, sems.at[sem]))
    for copy in copies:
        copy.start()
    return copies


def pack_kernel(count, *refs):
    arrays, out = refs[:count], refs[-1]
    for t in range(out.shape[0]):
        first = 0
        for array in arrays:
            columns = array.shape[1] // 8
            begin = (t % 8) * columns
            out[t, :, first : first + columns] = array[:, begin : begin + columns]
            first += columns


def pack(arrays, places):
    depth = arrays[0].shape[0]
    columns = sum(array.shape[1] for array in arrays) // 8
    vmem = pl.BlockSpec(memory_space=pltpu.VMEM)
    return pl.pallas_call(
        functools.partial(pack_kernel, len(arrays)),
        out_shape=jax.ShapeDtypeStruct((places, depth, columns), jnp.bfloat16),
        in_specs=[vmem] * len(arrays),
        out_specs=vmem,
        compiler_params=pltpu.CompilerParams(vmem_limit_bytes=VMEM_BYTES),
    )(*arrays)


def mix_kernel(out_weight, inputs, packed):
    rows = inputs.shape[0] // 8
    width = inputs.shape[1]
    for t in range(8):
        packed[t, :rows] = inputs[t * rows : (t + 1) * rows]
        packed[t, rows:] = out_weight[:, t * width : (t + 1) * width]


def mix(out_weight, inputs):
    batch, width = inputs.shape
    vmem = pl.BlockSpec(memory_space=pltpu.VMEM)
    return pl.pallas_call(
        mix_kernel,
        out_shape=jax.ShapeDtypeStruct((8, batch // 8 + out_weight.shape[0], width), jnp.bfloat16),
        in_specs=[vmem] * 2,
        out_specs=vmem,
        compiler_params=pltpu.CompilerParams(vmem_limit_bytes=VMEM_BYTES),
    )(out_weight, inputs)


def unpack_kernel(packed, gain, normed, out_weight):
    rows, width = normed.shape[2:]
    deep = out_weight.shape[0] // 8
    total = None
    for t in range(8):
        values = packed[t, :rows].astype(jnp.float32)
        squares = jnp.sum(values * values, axis=-1, keepdims=True)
        total = squares if total is None else total + squares
    factor = lax.rsqrt(total / (8 * width) + norm_eps)
    for t in range(8):
        values = packed[t, :rows].astype(jnp.float32) * factor
        values = values * gain[t : t + 1, :].astype(jnp.float32)
        normed[(t >> 2) * 2 + (t & 1), (t >> 1) & 1] = values.astype(jnp.bfloat16)
        out_weight[t * deep : (t + 1) * deep] = packed[t, rows:]


def unpack(packed, gain, rows):
    _, both, width = packed.shape
    vmem = pl.BlockSpec(memory_space=pltpu.VMEM)
    return pl.pallas_call(
        unpack_kernel,
        out_shape=[
            jax.ShapeDtypeStruct((4, 2, rows, width), jnp.bfloat16),
            jax.ShapeDtypeStruct((8 * (both - rows), width), jnp.bfloat16),
        ],
        in_specs=[vmem] * 2,
        out_specs=[vmem] * 2,
        compiler_params=pltpu.CompilerParams(vmem_limit_bytes=VMEM_BYTES),
    )(packed, gain)


def partial_kernel(place, *refs):
    blocks, weights, outs, acts, held, sums, sems, more = refs[:10], refs[10:12], refs[12:16], *refs[16:]

    width = blocks[0].shape[3]
    half = weights[0].shape[1]

    def spots(block, index, part, sem):
        return [
            (block.at[:, k], acts.at[part, index, :, pl.ds(k * width, width)], (sem, k)) for k in range(2)
        ]

    copies = settle(place, blocks, spots, sems)
    here, core = place[4] * 2 + place[0] % 2, place[1]
    for i in range(4):
        rows = pl.ds(pl.multiple_of(((i >> 1) * 2 + (core ^ (i & 1))) * half, half), half)
        copies.append(pltpu.make_async_copy(weights[i & 1].at[i >> 1], held.at[rows], more.at[i]))
        copies[-1].start()
    for copy in copies:
        copy.wait()
    batch = outs[0].shape[0]
    product = jnp.dot(acts[...].reshape(4 * batch, 2 * width), held[...], preferred_element_type=jnp.float32)
    sums[...] = product.astype(sums.dtype).reshape(sums.shape)
    for k in range(4):
        outs[k][...] = sums[here ^ k]


def partial_products(place, blocks, weights):
    _, _, rows, width = blocks[0].shape
    _, depth, columns = weights[0].shape
    vmem = pl.BlockSpec(memory_space=pltpu.VMEM)
    return pl.pallas_call(
        partial_kernel,
        out_shape=[jax.ShapeDtypeStruct((8 * rows, columns), jnp.bfloat16)] * 4,
        in_specs=[pl.BlockSpec(memory_space=pltpu.SMEM)] + [pl.BlockSpec(memory_space=pl.ANY)] * 12,
        out_specs=[vmem] * 4,
        scratch_shapes=[
            pltpu.VMEM((4, 8, rows, 2 * width), jnp.bfloat16),
            pltpu.VMEM((4 * depth, columns), jnp.bfloat16),
            pltpu.VMEM((4, 8 * rows, columns), jnp.bfloat16),
            pltpu.SemaphoreType.DMA((10, 2)),
            pltpu.SemaphoreType.DMA((4,)),
        ],
        compiler_params=pltpu.CompilerParams(vmem_limit_bytes=VMEM_BYTES),
        cost_estimate=pl.CostEstimate(
            flops=2 * 32 * rows * 2 * width * columns, bytes_accessed=8 * 1024 * 1024, transcendentals=0
        ),
    )(place, *blocks, *weights)


def output_kernel(place, *refs):
    blocks, weight, out, acts, sems = refs[:10], *refs[10:]
    width = blocks[0].shape[1]

    def spots(block, index, part, sem):
        columns = pl.ds(pl.multiple_of(index * width, width), width)
        return [(block, acts.at[part, columns], (sem,))]

    for copy in settle(place, blocks, spots, sems):
        copy.wait()
    out[...] = jnp.dot(acts[...], weight[...], preferred_element_type=jnp.float32).astype(out.dtype)


def output_product(place, blocks, weight):
    batch, width = blocks[0].shape
    columns = weight.shape[1]
    return pl.pallas_call(
        output_kernel,
        out_shape=jax.ShapeDtypeStruct((batch, columns), jnp.bfloat16),
        in_specs=[pl.BlockSpec(memory_space=pltpu.SMEM)]
        + [pl.BlockSpec(memory_space=pl.ANY)] * 10
        + [pl.BlockSpec(memory_space=pltpu.VMEM)],
        out_specs=pl.BlockSpec(memory_space=pltpu.VMEM),
        scratch_shapes=[
            pltpu.VMEM((batch, 8 * width), jnp.bfloat16),
            pltpu.SemaphoreType.DMA((10,)),
        ],
        compiler_params=pltpu.CompilerParams(vmem_limit_bytes=32 * 1024 * 1024),
        cost_estimate=pl.CostEstimate(
            flops=2 * batch * 8 * width * columns, bytes_accessed=10 * 1024 * 1024, transcendentals=0
        ),
    )(place, *blocks, weight)


def tie(block, *others):
    anywhere = pl.BlockSpec(memory_space=pl.ANY)

    def kernel(*refs):
        pass

    return pl.pallas_call(
        kernel,
        out_shape=jax.ShapeDtypeStruct(block.shape, block.dtype),
        in_specs=[anywhere] * (1 + len(others)),
        out_specs=anywhere,
        input_output_aliases={0: 0},
    )(block, *others)


def stage_kernel(count, arrays, *refs):
    sources, targets, sems = refs[:arrays], refs[count:-1], refs[-1]
    copies = []
    for i in range(arrays):
        pieces = sems.shape[1]
        size = sources[i].shape[0] // pieces
        for k in range(pieces):
            part = pl.ds(k * size, size)
            copies.append(pltpu.make_async_copy(sources[i].at[part], targets[i].at[part], sems.at[i, k]))
    for copy in copies:
        copy.start()
    for copy in copies:
        copy.wait()


def stage(arrays, *others):
    anywhere = pl.BlockSpec(memory_space=pl.ANY)
    count = len(arrays) + len(others)
    size = sum(array.size * array.dtype.itemsize for array in arrays)
    return pl.pallas_call(
        functools.partial(stage_kernel, count, len(arrays)),
        out_shape=[jax.ShapeDtypeStruct(array.shape, array.dtype) for array in arrays],
        in_specs=[anywhere] * count,
        out_specs=[anywhere] * len(arrays),
        scratch_shapes=[pltpu.SemaphoreType.DMA((len(arrays), 8))],
        compiler_params=pltpu.CompilerParams(vmem_limit_bytes=1024 * 1024),
        cost_estimate=pl.CostEstimate(flops=0, bytes_accessed=2 * size, transcendentals=0),
    )(*arrays, *others)


def attention_kernel(lengths, *refs):
    parts, (cosine, sine, key, value, out), scratch = refs[:4], refs[4:9], refs[9:]
    queries, fresh_keys, fresh_values, scores, sums = scratch
    rows, heads, _ = queries.shape
    chunk = scores.shape[0] // heads

    if True:
        projected = parts[0][...].astype(jnp.float32)
        for part in parts[1:]:
            projected = projected + part[...].astype(jnp.float32)

        def head(k):
            return projected[:, k * HD : (k + 1) * HD]

        def turned(vectors):
            moved = vectors * cosine[...] + pltpu.roll(vectors, HD // 2, 1) * sine[...]
            return moved.astype(jnp.bfloat16).astype(jnp.float32)

        for k in range(GROUP):
            query = turned(head(k))
            for s in range(STEPS):
                queries[:, s * GROUP + k, :] = query[s * rows : (s + 1) * rows]
        fresh_key = turned(head(GROUP))
        fresh_value = head(GROUP + 1).astype(jnp.bfloat16).astype(jnp.float32)
        for s in range(STEPS):
            fresh_keys[s] = fresh_key[s * rows : (s + 1) * rows]
            fresh_values[s] = fresh_value[s * rows : (s + 1) * rows]

    scale = HD ** (-0.5)
    at_step = lax.broadcasted_iota(jnp.int32, (chunk * heads, 1), 0) % heads // GROUP

    def repeated(vectors):
        return jnp.broadcast_to(vectors[:, None, :], (chunk, heads, HD)).reshape(chunk * heads, HD)

    def some_rows(step, carry):
        begin = pl.multiple_of(step * chunk, chunk)
        here = pl.ds(begin, chunk)
        query = queries[here].reshape(chunk * heads, HD)
        for r in range(chunk):
            scores[r * heads : (r + 1) * heads] = lax.dot_general(
                query[r * heads : (r + 1) * heads].astype(jnp.bfloat16),
                key[begin + r],
                (((1,), (1,)), ((), ())),
                preferred_element_type=jnp.float32,
            )
        cached = scores[...] * scale
        spot = lax.broadcasted_iota(jnp.int32, cached.shape, 1)
        limit = lengths[pl.ds(pl.multiple_of(step * chunk * heads, chunk * heads), chunk * heads)]
        cached = jnp.where(spot < limit, cached, -jnp.inf)
        new = []
        highest = jnp.max(cached, axis=-1, keepdims=True)
        for s in range(STEPS):
            score = jnp.sum(query * repeated(fresh_keys[s, here]), axis=-1, keepdims=True) * scale
            new.append(jnp.where(at_step >= s, score, -jnp.inf))
            highest = jnp.maximum(highest, new[s])
        cached = jnp.exp(cached - highest)
        new = [jnp.exp(score - highest) for score in new]
        total = jnp.sum(cached, axis=-1, keepdims=True) + new[0] + new[1]
        share = 1.0 / total
        scores[...] = cached * share
        result = None
        for s in range(STEPS):
            prob = (new[s] * share).astype(jnp.bfloat16).astype(jnp.float32)
            term = prob * repeated(fresh_values[s, here])
            result = term if result is None else result + term
        result = result.reshape(chunk, heads, HD)
        for r in range(chunk):
            prob = scores[r * heads : (r + 1) * heads].astype(jnp.bfloat16)
            sums[begin + r] = result[r] + jnp.dot(prob, value[begin + r], preferred_element_type=jnp.float32)
        return carry

    lax.fori_loop(0, rows // chunk, some_rows, 0)
    for s in range(STEPS):
        for k in range(GROUP):
            out[s * rows : (s + 1) * rows, k * HD : (k + 1) * HD] = sums[:, s * GROUP + k, :].astype(out.dtype)


def attention_of(parts, cosine, sine, key_cache, value_cache, lengths, chunk=8):
    batch, columns = parts[0].shape
    rows, spots, _ = key_cache.shape
    heads = STEPS * GROUP
    vmem = pl.BlockSpec(memory_space=pltpu.VMEM)
    return pl.pallas_call(
        attention_kernel,
        out_shape=jax.ShapeDtypeStruct((batch, GROUP * HD), jnp.bfloat16),
        in_specs=[vmem] * 9,
        out_specs=vmem,
        scratch_shapes=[
            pltpu.VMEM((rows, heads, HD), jnp.float32),
            pltpu.VMEM((STEPS, rows, HD), jnp.float32),
            pltpu.VMEM((STEPS, rows, HD), jnp.float32),
            pltpu.VMEM((chunk * heads, spots), jnp.float32),
            pltpu.VMEM((rows, heads, HD), jnp.float32),
        ],
        compiler_params=pltpu.CompilerParams(vmem_limit_bytes=32 * 1024 * 1024),
        cost_estimate=pl.CostEstimate(
            flops=4 * rows * heads * spots * HD,
            bytes_accessed=4 * rows * spots * HD,
            transcendentals=rows * heads * spots,
        ),
    )(jnp.repeat(lengths, heads)[:, None], *parts, cosine, sine, key_cache, value_cache)


def shards(step_inputs, norm_gain, w_query, w_key, w_value, w_out, key_cache, value_cache, lengths):
    steps, rows, width = step_inputs.shape
    batch = steps * rows
    place = jnp.stack(
        [
            lax.axis_index(("y1", "y0")),
            lax.axis_index("c"),
            lax.axis_index(("x1", "x0")),
            lax.axis_index("zl"),
            lax.axis_index("zh"),
        ]
    ).astype(jnp.int32)

    packed = mix(w_out, step_inputs.reshape(batch, width))
    packed = lax.all_to_all(packed, TP, 0, 0, tiled=True)
    normed, out_mine = unpack(packed, norm_gain.reshape(8, width), batch // 8)
    out_weight = lax.all_gather(out_mine, REP, axis=0, tiled=True)

    moved = lax.all_to_all(normed, SPLIT, 0, 0, tiled=True)
    gathered = ring_gather(moved, "zl", "x1", "x0")
    cut = tie(pack((w_query, w_key, w_value), 16), moved)
    mine = lax.all_to_all(cut, (REST,) + TP, 0, 0, tiled=True)
    mine = mine.reshape(2, 8 * cut.shape[1], cut.shape[2])
    mine = tie(mine, gathered[1], gathered[2], gathered[5])
    weights = (mine, permute(mine, flipped("c")))
    partial = partial_products(place, gathered, weights)
    caches = stage((key_cache[:, 0], value_cache[:, 0]), partial[0])
    changes = [flipped(SPLIT[0]), flipped(SPLIT[1])]
    parts = [
        partial[0],
        permute(partial[3], lambda bits: changes[0](changes[1](bits))),
        permute(partial[2], changes[0]),
        permute(partial[1], changes[1]),
    ]
    positions = (lengths[None, :] + jnp.arange(steps)[:, None]).reshape(batch)
    cosine, sine = turns(positions)
    attention = attention_of(
        parts, cosine, sine, *caches, lengths
    )
    joined = ring_gather(attention, "zl", "x1", "x0")
    out_weight = stage((out_weight,), attention)[0]
    result = output_product(place, joined, out_weight)
    return result.reshape(steps, rows, width)


def solution(mesh):
    fine = Mesh(mesh.devices.reshape((2,) * 7), AXES)
    in_specs = (
        P(None, REP, TP),
        P(),
        P(AXES, None),
        P(AXES, None),
        P(AXES, None),
        P(AXES, None),
        P(REP, TP, None, None),
        P(REP, TP, None, None),
        P(REP),
    )
    out_specs = P(None, REP, TP)
    return jax.shard_map(shards, mesh=fine, in_specs=in_specs, out_specs=out_specs, check_vma=False)
```

```python
import functools

import jax
import jax.numpy as jnp
from jax import lax
from jax.experimental import pallas as pl
from jax.experimental.pallas import tpu as pltpu
from jax.sharding import Mesh, PartitionSpec as P

HD = 128
STEPS = 2
GROUP = 4

VMEM_BYTES = 60 * 1024 * 1024

norm_eps = 1e-05
rope_base = 500000.0

AXES = ("zh", "y1", "y0", "c", "x1", "x0", "zl")
REP = ("zh", "y1", "y0", "c")
TP = ("x1", "x0", "zl")
SPLIT = ("zh", "y0")
REST = "y1"


def pairs_of(change):
    pairs = []
    for device in range(128):
        bits = {axis: (device >> (6 - i)) & 1 for i, axis in enumerate(AXES)}
        moved = change(dict(bits))
        pairs.append((device, sum(moved[axis] << (6 - i) for i, axis in enumerate(AXES))))
    return pairs


def flipped(axis):
    def change(bits):
        bits[axis] ^= 1
        return bits

    return change


def permute(block, change):
    return lax.ppermute(block, AXES, pairs_of(change))


def shifted(high, low, by):
    def change(bits):
        place = (bits[high] * 2 + bits[low] + by) % 4
        bits[high], bits[low] = place >> 1, place & 1
        return bits

    return change


def ring_gather(block, pair, high, low):
    half = block.shape[0] // 2
    up, down = shifted(high, low, 1), shifted(high, low, -1)
    mate = permute(block, flipped(pair))
    own_side = [block, permute(block, up), permute(block, down)]
    mate_side = [mate, permute(mate, up), permute(mate, down)]
    for side in (own_side, mate_side):
        side.append(permute(side[1][:half], up))
        side.append(permute(side[2][half:], down))
    return own_side + mate_side


def ring_places(mine):
    return [mine, (mine + 3) % 4, (mine + 1) % 4, (mine + 2) % 4]


def turns(positions):
    half = HD // 2
    ladder = jnp.arange(half).astype(jnp.float32)
    frequency = jnp.power(jnp.float32(rope_base), -2.0 * ladder / HD)
    angles = positions.astype(jnp.float32)[:, None] * frequency[None, :]
    cosine, sine = jnp.cos(angles), jnp.sin(angles)
    return jnp.concatenate([cosine, cosine], axis=-1), jnp.concatenate([-sine, sine], axis=-1)


def settle(place, blocks, spots, sems):
    ring, pair = place[2], place[3]
    half = blocks[3].shape[0]
    copies = []
    for side in range(2):
        for k, spot in enumerate(ring_places(ring)):
            index = spot * 2 + (pair ^ side)
            first = side * 5 + k
            for low in range(1 if k < 3 else 2):
                rows = pl.ds(low * half, half if k == 3 else 2 * half)
                for source, target, sem in spots(blocks[first + low], index, rows, first + low):
                    copies.append(pltpu.make_async_copy(source, target, sems.at[sem]))
    for copy in copies:
        copy.start()
    return copies


def pack_kernel(count, *refs):
    arrays, out = refs[:count], refs[-1]
    for t in range(out.shape[0]):
        first = 0
        for array in arrays:
            columns = array.shape[1] // 8
            begin = (t % 8) * columns
            out[t, :, first : first + columns] = array[:, begin : begin + columns]
            first += columns


def pack(arrays, places):
    depth = arrays[0].shape[0]
    columns = sum(array.shape[1] for array in arrays) // 8
    vmem = pl.BlockSpec(memory_space=pltpu.VMEM)
    return pl.pallas_call(
        functools.partial(pack_kernel, len(arrays)),
        out_shape=jax.ShapeDtypeStruct((places, depth, columns), jnp.bfloat16),
        in_specs=[vmem] * len(arrays),
        out_specs=vmem,
        compiler_params=pltpu.CompilerParams(vmem_limit_bytes=VMEM_BYTES),
    )(*arrays)


def mix_kernel(out_weight, inputs, packed, sems):
    rows = inputs.shape[0] // 8
    deep, width = out_weight.shape[0], inputs.shape[1]
    copies = []
    for t in range(8):
        mine = inputs.at[pl.ds(t * rows, rows)]
        cut = out_weight.at[:, pl.ds(t * width, width)]
        copies.append(pltpu.make_async_copy(mine, packed.at[t, pl.ds(0, rows)], sems.at[t, 0]))
        copies.append(pltpu.make_async_copy(cut, packed.at[t, pl.ds(rows, deep)], sems.at[t, 1]))
    for copy in copies:
        copy.start()
    for copy in copies:
        copy.wait()


def mix(out_weight, inputs):
    batch, width = inputs.shape
    anywhere = pl.BlockSpec(memory_space=pl.ANY)
    return pl.pallas_call(
        mix_kernel,
        out_shape=jax.ShapeDtypeStruct((8, batch // 8 + out_weight.shape[0], width), jnp.bfloat16),
        in_specs=[anywhere] * 2,
        out_specs=pl.BlockSpec(memory_space=pltpu.VMEM),
        scratch_shapes=[pltpu.SemaphoreType.DMA((8, 2))],
        compiler_params=pltpu.CompilerParams(vmem_limit_bytes=VMEM_BYTES),
    )(out_weight, inputs)


def unpack_kernel(packed, gain, normed, out_weight):
    rows, width = normed.shape[2:]
    deep = out_weight.shape[0] // 8
    total = None
    for t in range(8):
        values = packed[t, :rows].astype(jnp.float32)
        squares = jnp.sum(values * values, axis=-1, keepdims=True)
        total = squares if total is None else total + squares
    factor = lax.rsqrt(total / (8 * width) + norm_eps)
    for t in range(8):
        values = packed[t, :rows].astype(jnp.float32) * factor
        values = values * gain[t : t + 1, :].astype(jnp.float32)
        normed[(t >> 2) * 2 + (t & 1), (t >> 1) & 1] = values.astype(jnp.bfloat16)
        out_weight[t * deep : (t + 1) * deep] = packed[t, rows:]


def unpack(packed, gain, rows):
    _, both, width = packed.shape
    vmem = pl.BlockSpec(memory_space=pltpu.VMEM)
    return pl.pallas_call(
        unpack_kernel,
        out_shape=[
            jax.ShapeDtypeStruct((4, 2, rows, width), jnp.bfloat16),
            jax.ShapeDtypeStruct((8 * (both - rows), width), jnp.bfloat16),
        ],
        in_specs=[vmem] * 2,
        out_specs=[vmem] * 2,
        compiler_params=pltpu.CompilerParams(vmem_limit_bytes=VMEM_BYTES),
    )(packed, gain)


def partial_kernel(place, *refs):
    blocks, weights, outs, acts, held, sums, sems, more = refs[:10], refs[10:12], refs[12:16], *refs[16:]

    width = blocks[0].shape[3]
    half = weights[0].shape[1]

    def spots(block, index, part, sem):
        return [
            (block.at[:, k], acts.at[part, index, :, pl.ds(k * width, width)], (sem, k)) for k in range(2)
        ]

    copies = settle(place, blocks, spots, sems)
    here, core = place[4] * 2 + place[0] % 2, place[1]
    for i in range(4):
        rows = pl.ds(pl.multiple_of(((i >> 1) * 2 + (core ^ (i & 1))) * half, half), half)
        copies.append(pltpu.make_async_copy(weights[i & 1].at[i >> 1], held.at[rows], more.at[i]))
        copies[-1].start()
    for copy in copies:
        copy.wait()
    batch = outs[0].shape[0]
    product = jnp.dot(acts[...].reshape(4 * batch, 2 * width), held[...], preferred_element_type=jnp.float32)
    sums[...] = product.astype(sums.dtype).reshape(sums.shape)
    for k in range(4):
        outs[k][...] = sums[here ^ k]


def partial_products(place, blocks, weights):
    _, _, rows, width = blocks[0].shape
    _, depth, columns = weights[0].shape
    vmem = pl.BlockSpec(memory_space=pltpu.VMEM)
    return pl.pallas_call(
        partial_kernel,
        out_shape=[jax.ShapeDtypeStruct((8 * rows, columns), jnp.bfloat16)] * 4,
        in_specs=[pl.BlockSpec(memory_space=pltpu.SMEM)] + [pl.BlockSpec(memory_space=pl.ANY)] * 12,
        out_specs=[vmem] * 4,
        scratch_shapes=[
            pltpu.VMEM((4, 8, rows, 2 * width), jnp.bfloat16),
            pltpu.VMEM((4 * depth, columns), jnp.bfloat16),
            pltpu.VMEM((4, 8 * rows, columns), jnp.bfloat16),
            pltpu.SemaphoreType.DMA((10, 2)),
            pltpu.SemaphoreType.DMA((4,)),
        ],
        compiler_params=pltpu.CompilerParams(vmem_limit_bytes=VMEM_BYTES),
        cost_estimate=pl.CostEstimate(
            flops=2 * 32 * rows * 2 * width * columns, bytes_accessed=8 * 1024 * 1024, transcendentals=0
        ),
    )(place, *blocks, *weights)


def output_kernel(place, *refs):
    blocks, weight, out, acts, sems = refs[:10], *refs[10:]
    width = blocks[0].shape[1]

    def spots(block, index, part, sem):
        columns = pl.ds(pl.multiple_of(index * width, width), width)
        return [(block, acts.at[part, columns], (sem,))]

    for copy in settle(place, blocks, spots, sems):
        copy.wait()
    out[...] = jnp.dot(acts[...], weight[...], preferred_element_type=jnp.float32).astype(out.dtype)


def output_product(place, blocks, weight):
    batch, width = blocks[0].shape
    columns = weight.shape[1]
    return pl.pallas_call(
        output_kernel,
        out_shape=jax.ShapeDtypeStruct((batch, columns), jnp.bfloat16),
        in_specs=[pl.BlockSpec(memory_space=pltpu.SMEM)]
        + [pl.BlockSpec(memory_space=pl.ANY)] * 10
        + [pl.BlockSpec(memory_space=pltpu.VMEM)],
        out_specs=pl.BlockSpec(memory_space=pltpu.VMEM),
        scratch_shapes=[
            pltpu.VMEM((batch, 8 * width), jnp.bfloat16),
            pltpu.SemaphoreType.DMA((10,)),
        ],
        compiler_params=pltpu.CompilerParams(vmem_limit_bytes=32 * 1024 * 1024),
        cost_estimate=pl.CostEstimate(
            flops=2 * batch * 8 * width * columns, bytes_accessed=10 * 1024 * 1024, transcendentals=0
        ),
    )(place, *blocks, weight)


def tie(block, *others):
    anywhere = pl.BlockSpec(memory_space=pl.ANY)

    def kernel(*refs):
        pass

    return pl.pallas_call(
        kernel,
        out_shape=jax.ShapeDtypeStruct(block.shape, block.dtype),
        in_specs=[anywhere] * (1 + len(others)),
        out_specs=anywhere,
        input_output_aliases={0: 0},
    )(block, *others)


def stage_kernel(count, arrays, *refs):
    sources, targets, sems = refs[:arrays], refs[count:-1], refs[-1]
    copies = []
    for i in range(arrays):
        pieces = sems.shape[1]
        size = sources[i].shape[0] // pieces
        for k in range(pieces):
            part = pl.ds(k * size, size)
            copies.append(pltpu.make_async_copy(sources[i].at[part], targets[i].at[part], sems.at[i, k]))
    for copy in copies:
        copy.start()
    for copy in copies:
        copy.wait()


def stage(arrays, *others):
    anywhere = pl.BlockSpec(memory_space=pl.ANY)
    count = len(arrays) + len(others)
    size = sum(array.size * array.dtype.itemsize for array in arrays)
    return pl.pallas_call(
        functools.partial(stage_kernel, count, len(arrays)),
        out_shape=[jax.ShapeDtypeStruct(array.shape, array.dtype) for array in arrays],
        in_specs=[anywhere] * count,
        out_specs=[anywhere] * len(arrays),
        scratch_shapes=[pltpu.SemaphoreType.DMA((len(arrays), 8))],
        compiler_params=pltpu.CompilerParams(vmem_limit_bytes=1024 * 1024),
        cost_estimate=pl.CostEstimate(flops=0, bytes_accessed=2 * size, transcendentals=0),
    )(*arrays, *others)


def attention_kernel(lengths, *refs):
    parts, (cosine, sine, key, value, out), scratch = refs[:4], refs[4:9], refs[9:]
    queries, fresh_keys, fresh_values, scores, sums = scratch
    rows, heads, _ = queries.shape
    chunk = scores.shape[0] // heads

    if True:
        projected = parts[0][...].astype(jnp.float32)
        for part in parts[1:]:
            projected = projected + part[...].astype(jnp.float32)

        def head(k):
            return projected[:, k * HD : (k + 1) * HD]

        def turned(vectors):
            moved = vectors * cosine[...] + pltpu.roll(vectors, HD // 2, 1) * sine[...]
            return moved.astype(jnp.bfloat16).astype(jnp.float32)

        for k in range(GROUP):
            query = turned(head(k))
            for s in range(STEPS):
                queries[:, s * GROUP + k, :] = query[s * rows : (s + 1) * rows]
        fresh_key = turned(head(GROUP))
        fresh_value = head(GROUP + 1).astype(jnp.bfloat16).astype(jnp.float32)
        for s in range(STEPS):
            fresh_keys[s] = fresh_key[s * rows : (s + 1) * rows]
            fresh_values[s] = fresh_value[s * rows : (s + 1) * rows]

    scale = HD ** (-0.5)
    at_step = lax.broadcasted_iota(jnp.int32, (chunk * heads, 1), 0) % heads // GROUP

    def repeated(vectors):
        return jnp.broadcast_to(vectors[:, None, :], (chunk, heads, HD)).reshape(chunk * heads, HD)

    def some_rows(step, carry):
        begin = pl.multiple_of(step * chunk, chunk)
        here = pl.ds(begin, chunk)
        query = queries[here].reshape(chunk * heads, HD)
        for r in range(chunk):
            scores[r * heads : (r + 1) * heads] = lax.dot_general(
                query[r * heads : (r + 1) * heads].astype(jnp.bfloat16),
                key[begin + r],
                (((1,), (1,)), ((), ())),
                preferred_element_type=jnp.float32,
            )
        cached = scores[...] * scale
        spot = lax.broadcasted_iota(jnp.int32, cached.shape, 1)
        limit = lengths[pl.ds(pl.multiple_of(step * chunk * heads, chunk * heads), chunk * heads)]
        cached = jnp.where(spot < limit, cached, -jnp.inf)
        new = []
        highest = jnp.max(cached, axis=-1, keepdims=True)
        for s in range(STEPS):
            score = jnp.sum(query * repeated(fresh_keys[s, here]), axis=-1, keepdims=True) * scale
            new.append(jnp.where(at_step >= s, score, -jnp.inf))
            highest = jnp.maximum(highest, new[s])
        cached = jnp.exp(cached - highest)
        new = [jnp.exp(score - highest) for score in new]
        total = jnp.sum(cached, axis=-1, keepdims=True) + new[0] + new[1]
        share = 1.0 / total
        scores[...] = cached * share
        result = None
        for s in range(STEPS):
            prob = (new[s] * share).astype(jnp.bfloat16).astype(jnp.float32)
            term = prob * repeated(fresh_values[s, here])
            result = term if result is None else result + term
        result = result.reshape(chunk, heads, HD)
        for r in range(chunk):
            prob = scores[r * heads : (r + 1) * heads].astype(jnp.bfloat16)
            sums[begin + r] = result[r] + jnp.dot(prob, value[begin + r], preferred_element_type=jnp.float32)
        return carry

    lax.fori_loop(0, rows // chunk, some_rows, 0)
    for s in range(STEPS):
        for k in range(GROUP):
            out[s * rows : (s + 1) * rows, k * HD : (k + 1) * HD] = sums[:, s * GROUP + k, :].astype(out.dtype)


def attention_of(parts, cosine, sine, key_cache, value_cache, lengths, chunk=64):
    batch, columns = parts[0].shape
    rows, spots, _ = key_cache.shape
    heads = STEPS * GROUP
    vmem = pl.BlockSpec(memory_space=pltpu.VMEM)
    return pl.pallas_call(
        attention_kernel,
        out_shape=jax.ShapeDtypeStruct((batch, GROUP * HD), jnp.bfloat16),
        in_specs=[vmem] * 9,
        out_specs=vmem,
        scratch_shapes=[
            pltpu.VMEM((rows, heads, HD), jnp.float32),
            pltpu.VMEM((STEPS, rows, HD), jnp.float32),
            pltpu.VMEM((STEPS, rows, HD), jnp.float32),
            pltpu.VMEM((chunk * heads, spots), jnp.float32),
            pltpu.VMEM((rows, heads, HD), jnp.float32),
        ],
        compiler_params=pltpu.CompilerParams(vmem_limit_bytes=32 * 1024 * 1024),
        cost_estimate=pl.CostEstimate(
            flops=4 * rows * heads * spots * HD,
            bytes_accessed=4 * rows * spots * HD,
            transcendentals=rows * heads * spots,
        ),
    )(jnp.repeat(lengths, heads)[:, None], *parts, cosine, sine, key_cache, value_cache)


def shards(step_inputs, norm_gain, w_query, w_key, w_value, w_out, key_cache, value_cache, lengths):
    steps, rows, width = step_inputs.shape
    batch = steps * rows
    place = jnp.stack(
        [
            lax.axis_index(("y1", "y0")),
            lax.axis_index("c"),
            lax.axis_index(("x1", "x0")),
            lax.axis_index("zl"),
            lax.axis_index("zh"),
        ]
    ).astype(jnp.int32)

    packed = mix(w_out, step_inputs.reshape(batch, width))
    packed = lax.all_to_all(packed, TP, 0, 0, tiled=True)
    normed, out_mine = unpack(packed, norm_gain.reshape(8, width), batch // 8)
    out_weight = lax.all_gather(out_mine, REP, axis=0, tiled=True)

    moved = lax.all_to_all(normed, SPLIT, 0, 0, tiled=True)
    gathered = ring_gather(moved, "zl", "x1", "x0")
    cut = tie(pack((w_query, w_key, w_value), 16), moved)
    mine = lax.all_to_all(cut, (REST,) + TP, 0, 0, tiled=True)
    mine = mine.reshape(2, 8 * cut.shape[1], cut.shape[2])
    mine = tie(mine, gathered[1], gathered[2], gathered[5])
    weights = (mine, permute(mine, flipped("c")))
    partial = partial_products(place, gathered, weights)
    caches = stage((key_cache[:, 0], value_cache[:, 0]), partial[0])
    changes = [flipped(SPLIT[0]), flipped(SPLIT[1])]
    parts = [
        partial[0],
        permute(partial[3], lambda bits: changes[0](changes[1](bits))),
        permute(partial[2], changes[0]),
        permute(partial[1], changes[1]),
    ]
    positions = (lengths[None, :] + jnp.arange(steps)[:, None]).reshape(batch)
    cosine, sine = turns(positions)
    attention = attention_of(
        parts, cosine, sine, *caches, lengths
    )
    joined = ring_gather(attention, "zl", "x1", "x0")
    out_weight = stage((out_weight,), attention)[0]
    result = output_product(place, joined, out_weight)
    return result.reshape(steps, rows, width)


def solution(mesh):
    fine = Mesh(mesh.devices.reshape((2,) * 7), AXES)
    in_specs = (
        P(None, REP, TP),
        P(),
        P(AXES, None),
        P(AXES, None),
        P(AXES, None),
        P(AXES, None),
        P(REP, TP, None, None),
        P(REP, TP, None, None),
        P(REP),
    )
    out_specs = P(None, REP, TP)
    return jax.shard_map(shards, mesh=fine, in_specs=in_specs, out_specs=out_specs, check_vma=False)
```
